512 devices in a mesh: seg: 32 (over z_lo, y, core), dev: 16 (over z_hi, x).
Axes of the slice: x: 4, y: 4, z: 16 (z_hi: 4, z_lo: 4; z = z_hi * 4 + z_lo), core: 2. Of those that a mesh axis runs over, the one named last changes fastest.
Arguments:
- queries: bfloat16 [65536, 1536], P(('seg', 'dev')), may hold values from -12 to 12
- keys: bfloat16 [65536, 1536], P(('seg', 'dev')), may hold values from -12 to 12
- values: bfloat16 [65536, 1536], P(('seg', 'dev')), may hold values from -4 to 4
Outputs:
- grad_queries: bfloat16 [65536, 1536], P(('seg', 'dev'))
- grad_keys: bfloat16 [65536, 1536], P(('seg', 'dev'))
- grad_values: bfloat16 [65536, 1536], P(('seg', 'dev'))
The draws below stay inside these ranges and needn't reach their ends.
All inputs are finite; a program needn't handle non-finite values.
Results may differ from the reference program's by a relative error of at most 0.015.
Values may be sent and summed in bfloat16 or wider, within the bound.
A program may use at most 128 MiB of HBM per device.

```python
import jax
import jax.numpy as jnp
from jax import lax

D = 1536
HEADS = 16
WINDOW = 256
FR_DEV = 128
SEG = 2048
FRAMES = 65536
N_SEG = 32


def drawn_pair(key):
    query_base = jnp.clip(jax.random.normal(jax.random.fold_in(key, 11), (FRAMES, D), jnp.float32), -4.0, 4.0)
    key_base = jnp.clip(jax.random.normal(jax.random.fold_in(key, 12), (FRAMES, D), jnp.float32), -4.0, 4.0)
    return (query_base, key_base)


def draw_queries(key, part):
    return drawn_pair(key)[0].astype(jnp.bfloat16)


def draw_keys(key, part):
    return drawn_pair(key)[1].astype(jnp.bfloat16)


def levels(rng, shape, split, smallest, top_value):
    gain = 1.0
    for axis_at, shards_of in split:
        heights = jax.random.uniform(jax.random.fold_in(jax.random.fold_in(rng, 6), axis_at), (shards_of,), jnp.float32, smallest / len(split), top_value / len(split))
        gain = gain * jnp.repeat(jnp.exp(heights), shape[axis_at] // shards_of).reshape((-1,) + (1,) * (len(shape) - 1 - axis_at))
    return gain


def gaussian(own_key, dims, width, reach, cuts=(), kind=jnp.bfloat16):
    entries = width * jax.random.normal(own_key, dims, jnp.float32)
    if cuts:
        entries = entries * levels(own_key, dims, cuts, -0.22, 0.18)
    return jnp.clip(entries, -reach, reach).astype(kind)


def setup_inputs(seed: int = 0) -> dict:
    streams_of = jax.random.split(jax.random.key(seed), 4)
    queries = draw_queries(jax.random.fold_in(streams_of[3], 71), 0)
    keys = draw_keys(jax.random.fold_in(streams_of[3], 71), 0)
    values = gaussian(streams_of[2], (FRAMES, D), 1.0, 4.0, ((0, 512),))
    return {"queries": queries, "keys": keys, "values": values}


def student_pass(block_q, ext_keys, ext_values, target, first_row):
    row_count, model_width = block_q.shape
    ext_count = ext_keys.shape[0]
    reach_rows = ext_count - row_count
    head_dim = model_width // HEADS
    factor = head_dim ** -0.5
    query_heads = block_q.reshape(row_count, HEADS, head_dim).astype(jnp.float32)
    key_heads = ext_keys.reshape(ext_count, HEADS, head_dim).astype(jnp.float32)
    value_heads = ext_values.reshape(ext_count, HEADS, head_dim).astype(jnp.float32)
    scores = jnp.einsum("fhd,ehd->hfe", query_heads, key_heads) * factor
    query_pos = first_row + lax.iota(jnp.int32, row_count)
    key_pos = first_row - reach_rows + lax.iota(jnp.int32, ext_count)
    allowed = (key_pos[None, :] <= query_pos[:, None]) & (key_pos[None, :] >= query_pos[:, None] - reach_rows) & (key_pos[None, :] >= 0)
    scores = jnp.where(allowed[None], scores, -1e30)
    row_max = scores.max(-1, keepdims=True)
    numerators = jnp.exp(scores - row_max)
    probability = numerators / numerators.sum(-1, keepdims=True)
    weights = probability.astype(jnp.bfloat16).astype(jnp.float32)
    output = jnp.einsum("hfe,ehd->fhd", weights, value_heads).reshape(row_count, model_width)
    d_out = (128.0 * (output - target.astype(jnp.float32))).astype(jnp.bfloat16)
    d_out = d_out.astype(jnp.float32).reshape(row_count, HEADS, head_dim)
    grad_v = jnp.einsum("hfe,fhd->ehd", weights, d_out)
    d_prob = jnp.einsum("fhd,ehd->hfe", d_out, value_heads)
    row_inner = (probability * d_prob).sum(-1, keepdims=True)
    d_scores = (probability * (d_prob - row_inner) * factor).astype(jnp.bfloat16).astype(jnp.float32)
    grad_q = jnp.einsum("hfe,ehd->fhd", d_scores, key_heads)
    grad_k = jnp.einsum("hfe,fhd->ehd", d_scores, query_heads)
    return (grad_q.reshape(row_count, model_width), grad_k.reshape(ext_count, model_width), grad_v.reshape(ext_count, model_width))


def round_far(grad_rows):
    far_rows = lax.optimization_barrier(grad_rows[:WINDOW].astype(jnp.bfloat16)).astype(jnp.float32)
    return jnp.concatenate([far_rows, grad_rows[WINDOW:]], 0)


def teacher_block(query_block, seg_keys, seg_values):
    block_rows = query_block.shape[0]
    head_dim = D // HEADS
    factor = head_dim ** -0.5
    query_heads = query_block.reshape(block_rows, HEADS, head_dim).astype(jnp.float32)
    key_heads = seg_keys.reshape(-1, HEADS, head_dim).astype(jnp.float32)
    value_heads = seg_values.reshape(-1, HEADS, head_dim).astype(jnp.float32)
    scores = jnp.einsum("fhd,khd->hfk", query_heads, key_heads) * factor
    numerators = jnp.exp(scores - scores.max(-1, keepdims=True))
    totals = numerators.sum(-1, keepdims=True)
    weighted = jnp.einsum("hfk,khd->fhd", numerators.astype(jnp.bfloat16).astype(jnp.float32), value_heads)
    result = weighted / jnp.transpose(totals, (1, 0, 2))
    return result.reshape(block_rows, D).astype(jnp.bfloat16)


def teacher_segment(segment):
    seg_q, seg_k, seg_v = segment
    block_rows = 512 if SEG % 512 == 0 else SEG
    blocks = seg_q.reshape(SEG // block_rows, block_rows, D)
    outputs = lax.map(lambda query_block: teacher_block(query_block, seg_k, seg_v), blocks)
    return outputs.reshape(SEG, D)


def reference(queries, keys, values):
    target = lax.map(teacher_segment, (queries.reshape(N_SEG, SEG, D), keys.reshape(N_SEG, SEG, D), values.reshape(N_SEG, SEG, D)))
    target = target.reshape(FRAMES, D)
    zero_rows = jnp.zeros((WINDOW, D), keys.dtype)
    key_pad = jnp.concatenate([zero_rows, keys], 0)
    value_pad = jnp.concatenate([zero_rows, values], 0)
    ext_count = WINDOW + FR_DEV

    def advance(state_now, block_index):
        grad_k_pad, grad_v_pad = state_now
        first_row = (block_index * FR_DEV).astype(jnp.int32)
        block_q = lax.dynamic_slice_in_dim(queries, first_row, FR_DEV, 0)
        block_t = lax.dynamic_slice_in_dim(target, first_row, FR_DEV, 0)
        ext_keys = lax.dynamic_slice_in_dim(key_pad, first_row, ext_count, 0)
        ext_values = lax.dynamic_slice_in_dim(value_pad, first_row, ext_count, 0)
        grad_q, grad_k, grad_v = student_pass(block_q, ext_keys, ext_values, block_t, first_row)
        grad_k = round_far(grad_k)
        grad_v = round_far(grad_v)
        new_k = lax.dynamic_slice_in_dim(grad_k_pad, first_row, ext_count, 0) + grad_k
        new_v = lax.dynamic_slice_in_dim(grad_v_pad, first_row, ext_count, 0) + grad_v
        grad_k_pad = lax.dynamic_update_slice_in_dim(grad_k_pad, new_k, first_row, 0)
        grad_v_pad = lax.dynamic_update_slice_in_dim(grad_v_pad, new_v, first_row, 0)
        return (grad_k_pad, grad_v_pad), grad_q.astype(jnp.bfloat16)

    start_state = (jnp.zeros((WINDOW + FRAMES, D), jnp.float32), jnp.zeros((WINDOW + FRAMES, D), jnp.float32))
    final_state, grad_rows = lax.scan(advance, start_state, jnp.arange(FRAMES // FR_DEV, dtype=jnp.int32))
    grad_queries = grad_rows.reshape(FRAMES, D)
    grad_keys = final_state[0][WINDOW:].astype(jnp.bfloat16)
    grad_values = final_state[1][WINDOW:].astype(jnp.bfloat16)
    return (grad_queries, grad_keys, grad_values)
```

```python
import functools

import jax
import jax.numpy as jnp
from jax import lax
from jax.experimental import pallas as pl
from jax.experimental.pallas import tpu as pltpu
from jax.sharding import PartitionSpec as P

HEADS = 16
WINDOW = 256
MESH = pl.DeviceIdType.MESH
F32 = jnp.float32
BF16 = jnp.bfloat16
LOG2E = 1.4426950408889634
CONTRACT_LANES = (((1,), (1,)), ((), ()))


def transposed(tile):
    return tile.astype(F32).T.astype(BF16)


def kernel(
    n_dev,
    n_seg,
    q_ref,
    k_ref,
    v_ref,
    gq_ref,
    gk_ref,
    gv_ref,
    send,
    recv,
    halo,
    feat,
    rows,
    acc,
    far_out,
    far_in,
    out_send,
    out_recv,
    in_ssem,
    in_rsem,
    halo_ssem,
    halo_rsem,
    far_ssem,
    far_rsem,
    out_ssem,
    out_rsem,
):
    me = lax.axis_index("dev")
    seg = lax.axis_index("seg")
    frames, width = q_ref.shape
    dim = width // n_dev
    far_blocks = WINDOW // frames
    segment = n_dev * frames
    ext = WINDOW + frames
    factor = dim ** (-0.5)
    next_seg = lax.rem(seg + 1, n_seg)
    prev_seg = lax.rem(seg + n_seg - 1, n_seg)
    tiles = width // 128

    def head_rows(d):
        return pl.ds(pl.multiple_of(d * dim, 32), dim)

    def frame_cols(block, count):
        return pl.ds(pl.multiple_of(block * frames, 128), count)

    barrier = pltpu.get_barrier_semaphore()
    for i in range(1, n_dev):
        pl.semaphore_signal(
            barrier, inc=1, device_id={"dev": lax.rem(me + i, n_dev)}, device_id_type=MESH
        )
    pl.semaphore_signal(barrier, inc=1, device_id={"seg": next_seg}, device_id_type=MESH)
    pl.semaphore_signal(barrier, inc=1, device_id={"seg": prev_seg}, device_id_type=MESH)

    def to_features(ref, a):
        for t in range(tiles):
            send[a, t * 128 : (t + 1) * 128, :] = transposed(ref[:, t * 128 : (t + 1) * 128])
        recv[a, me] = send[a, head_rows(me), :]

    def in_copy(a, d, slot, sem_at):
        return pltpu.make_async_remote_copy(
            src_ref=send.at[a, head_rows(d)],
            dst_ref=recv.at[a, slot],
            send_sem=in_ssem.at[a, d],
            recv_sem=in_rsem.at[a, sem_at],
            device_id={"dev": d},
            device_id_type=MESH,
        )

    def send_in(a):
        def body(i, carry):
            d = lax.rem(me + i, n_dev)
            in_copy(a, d, me, me).start()
            return carry

        lax.fori_loop(1, n_dev, body, 0)

    to_features(k_ref, 1)
    to_features(v_ref, 2)
    pl.semaphore_wait(barrier, n_dev + 1)
    send_in(1)
    send_in(2)
    to_features(q_ref, 0)
    send_in(0)

    acc[...] = jnp.zeros_like(acc)

    def place(a, block, piece):
        feat[a - 1, :, frame_cols(block, frames)] = piece
        rows[a - 1, frame_cols(block, frames), :] = transposed(piece)

    def gather(i, carry):
        src = lax.rem(me - i + n_dev, n_dev)
        for a in (1, 2):

            @pl.when(i > 0)
            def _():
                in_copy(a, src, src, src).wait_recv()

            place(a, src + far_blocks, recv[a, src])
        return carry

    lax.fori_loop(0, n_dev, gather, 0)

    def halo_copy(a):
        return pltpu.make_async_remote_copy(
            src_ref=recv.at[a, pl.ds(n_dev - far_blocks, far_blocks)],
            dst_ref=halo.at[a - 1],
            send_sem=halo_ssem.at[a - 1],
            recv_sem=halo_rsem.at[a - 1],
            device_id={"seg": next_seg},
            device_id_type=MESH,
        )

    for a in (1, 2):
        halo_copy(a).start()
    for a in (1, 2):
        halo_copy(a).wait_recv()
        for b in range(far_blocks):
            place(a, b, halo[a - 1, b])

    def out_copy(a, d, sem_at, head):
        return pltpu.make_async_remote_copy(
            src_ref=out_send.at[a, d],
            dst_ref=out_recv.at[a, head_rows(head)],
            send_sem=out_ssem.at[a, d],
            recv_sem=out_rsem.at[a, sem_at],
            device_id={"dev": d},
            device_id_type=MESH,
        )

    def give(a, block, value):
        @pl.when(block == me)
        def _():
            out_recv[a, head_rows(me), :] = value

        @pl.when(block != me)
        def _():
            out_send[a, block] = value
            out_copy(a, block, me, me).start()

    def give_keys(block):
        for a in (1, 2):
            give(a, block, acc[a - 1, block + far_blocks].astype(BF16))

    def far_copy():
        return pltpu.make_async_remote_copy(
            src_ref=far_out,
            dst_ref=far_in,
            send_sem=far_ssem,
            recv_sem=far_rsem,
            device_id={"seg": prev_seg},
            device_id_type=MESH,
        )

    key_at = lax.broadcasted_iota(jnp.int32, (ext, frames), 0)
    query_at = lax.broadcasted_iota(jnp.int32, (ext, frames), 1)
    in_window = (key_at >= query_at) & (key_at <= query_at + WINDOW)

    def one_block(s, carry):
        block = lax.rem(me - s + n_dev, n_dev)

        @pl.when(s > 0)
        def _():
            in_copy(0, block, block, block).wait_recv()

        q_feat = recv[0, block]
        scores = jnp.dot(
            rows[0, WINDOW : WINDOW + segment, :], q_feat, preferred_element_type=F32
        ) * (factor * LOG2E)
        numer = jnp.exp2(scores - scores.max(0, keepdims=True))
        total = numer.sum(0, keepdims=True)
        summed = jnp.dot(
            feat[1, :, WINDOW : WINDOW + segment], numer.astype(BF16), preferred_element_type=F32
        )
        target = (summed / total).astype(BF16).astype(F32)

        span = frame_cols(block, ext)
        first = (seg * n_dev + block) * frames - WINDOW
        allowed = in_window & (key_at + first >= 0)
        near = jnp.dot(rows[0, span, :], q_feat, preferred_element_type=F32) * (factor * LOG2E)
        near = jnp.where(allowed, near, -1e30)
        near_numer = jnp.exp2(near - near.max(0, keepdims=True))
        prob = near_numer / near_numer.sum(0, keepdims=True)
        weights = prob.astype(BF16)
        student = jnp.dot(feat[1, :, span], weights, preferred_element_type=F32)
        d_out = (128.0 * (student - target)).astype(BF16)
        d_prob = jnp.dot(rows[1, span, :], d_out, preferred_element_type=F32)
        inner = (prob * d_prob).sum(0, keepdims=True)
        d_scores = (prob * (d_prob - inner) * factor).astype(BF16)
        grad_q = jnp.dot(feat[0, :, span], d_scores, preferred_element_type=F32)
        grad_k = lax.dot_general(q_feat, d_scores, CONTRACT_LANES, preferred_element_type=F32)
        grad_v = lax.dot_general(d_out, weights, CONTRACT_LANES, preferred_element_type=F32)
        for b in range(far_blocks + 1):
            cols = slice(b * frames, (b + 1) * frames)
            acc[0, block + b] += grad_k[:, cols]
            acc[1, block + b] += grad_v[:, cols]
        give(0, block, grad_q.astype(BF16))

        last_first = jnp.where(me >= far_blocks - 1, 0, me + 1)

        @pl.when(block == last_first)
        def _():
            far_out[...] = acc[:, 0:far_blocks].astype(BF16)
            far_copy().start()

        @pl.when((s >= far_blocks) & (block < n_dev - far_blocks))
        def _():
            give_keys(block)

        return carry

    lax.fori_loop(0, n_dev, one_block, 0)

    for s in range(far_blocks):
        block = lax.rem(me - s + n_dev, n_dev)

        @pl.when(block < n_dev - far_blocks)
        def _():
            give_keys(block)

    far_copy().wait_recv()
    for b in range(far_blocks):
        for a in range(2):
            acc[a, n_dev + b] += far_in[a, b].astype(F32)
        give_keys(n_dev - far_blocks + b)

    group = 384 // dim
    for a, out in ((0, gq_ref), (1, gk_ref), (2, gv_ref)):
        for g in range(n_dev // group):
            for i in range(group):
                head = g * group + i

                @pl.when(head != me)
                def _():
                    out_copy(a, head, head, head).wait_recv()

            for t in range(3 * g, 3 * g + 3):
                cols = slice(t * 128, (t + 1) * 128)
                out[:, cols] = transposed(out_recv[a, cols, :])

    def drain(i, carry):
        d = lax.rem(me + i, n_dev)
        for a in range(3):
            in_copy(a, d, me, me).wait_send()
            out_copy(a, d, me, me).wait_send()
        return carry

    lax.fori_loop(1, n_dev, drain, 0)
    for a in (1, 2):
        halo_copy(a).wait_send()
    far_copy().wait_send()


def local(n_dev, n_seg, queries, keys, values):
    frames, width = queries.shape
    dim = width // n_dev
    far_blocks = WINDOW // frames
    held = n_dev + far_blocks
    vmem = pl.BlockSpec(memory_space=pltpu.VMEM)
    dma = pltpu.SemaphoreType.DMA
    return pl.pallas_call(
        functools.partial(kernel, n_dev, n_seg),
        out_shape=[jax.ShapeDtypeStruct((frames, width), BF16)] * 3,
        in_specs=[vmem] * 3,
        out_specs=[vmem] * 3,
        scratch_shapes=[
            pltpu.VMEM((3, width, frames), BF16),
            pltpu.VMEM((3, n_dev, dim, frames), BF16),
            pltpu.VMEM((2, far_blocks, dim, frames), BF16),
            pltpu.VMEM((2, dim, held * frames), BF16),
            pltpu.VMEM((2, held * frames, dim), BF16),
            pltpu.VMEM((2, held, dim, frames), F32),
            pltpu.VMEM((2, far_blocks, dim, frames), BF16),
            pltpu.VMEM((2, far_blocks, dim, frames), BF16),
            pltpu.VMEM((3, n_dev, dim, frames), BF16),
            pltpu.VMEM((3, width, frames), BF16),
            dma((3, n_dev)),
            dma((3, n_dev)),
            dma((2,)),
            dma((2,)),
            dma,
            dma,
            dma((3, n_dev)),
            dma((3, n_dev)),
        ],
        compiler_params=pltpu.CompilerParams(
            collective_id=0, has_side_effects=True, vmem_limit_bytes=48 << 20
        ),
        name="heads_exchange",
    )(queries, keys, values)


def solution(mesh):
    n_dev, n_seg = mesh.shape["dev"], mesh.shape["seg"]
    rows = P(("seg", "dev"), None)
    return jax.shard_map(
        functools.partial(local, n_dev, n_seg),
        mesh=mesh,
        in_specs=(rows, rows, rows),
        out_specs=(rows, rows, rows),
        check_vma=False,
    )
```

```python
import functools

import jax
import jax.numpy as jnp
from jax import lax
from jax.experimental import pallas as pl
from jax.experimental.pallas import tpu as pltpu
from jax.sharding import PartitionSpec as P

HEADS = 16
WINDOW = 256
MESH = pl.DeviceIdType.MESH
F32 = jnp.float32
BF16 = jnp.bfloat16
LOG2E = 1.4426950408889634
CONTRACT_LANES = (((1,), (1,)), ((), ()))


def transposed(tile):
    return tile.T


def kernel(
    n_dev,
    n_seg,
    q_ref,
    k_ref,
    v_ref,
    gq_ref,
    gk_ref,
    gv_ref,
    held_in,
    send,
    recv,
    halo,
    feat,
    rows,
    acc,
    far_out,
    far_in,
    out_send,
    out_recv,
    in_ssem,
    in_rsem,
    halo_ssem,
    halo_rsem,
    far_ssem,
    far_rsem,
    out_ssem,
    out_rsem,
    load_sem,
):
    me = lax.axis_index("dev")
    seg = lax.axis_index("seg")
    frames, width = q_ref.shape
    loads = [
        pltpu.make_async_copy(ref, held_in.at[a], load_sem.at[a])
        for a, ref in ((0, q_ref), (1, k_ref), (2, v_ref))
    ]
    for a in (1, 2, 0):
        loads[a].start()
    dim = width // n_dev
    far_blocks = WINDOW // frames
    segment = n_dev * frames
    ext = WINDOW + frames
    factor = dim ** (-0.5)
    next_seg = lax.rem(seg + 1, n_seg)
    prev_seg = lax.rem(seg + n_seg - 1, n_seg)
    tiles = width // 128

    def head_rows(d):
        return pl.ds(pl.multiple_of(d * dim, 32), dim)

    def frame_cols(block, count):
        return pl.ds(pl.multiple_of(block * frames, 128), count)

    barrier = pltpu.get_barrier_semaphore()
    for i in range(1, n_dev):
        pl.semaphore_signal(
            barrier, inc=1, device_id={"dev": lax.rem(me + i, n_dev)}, device_id_type=MESH
        )
    pl.semaphore_signal(barrier, inc=1, device_id={"seg": next_seg}, device_id_type=MESH)
    pl.semaphore_signal(barrier, inc=1, device_id={"seg": prev_seg}, device_id_type=MESH)

    def to_features(a):
        loads[a].wait()
        for t in range(tiles):
            cols = slice(t * 128, (t + 1) * 128)
            send[a, cols, :] = transposed(held_in[a, :, cols])
        recv[a, me] = send[a, head_rows(me), :]

    def in_copy(a, d, slot, sem_at):
        return pltpu.make_async_remote_copy(
            src_ref=send.at[a, head_rows(d)],
            dst_ref=recv.at[a, slot],
            send_sem=in_ssem.at[a, d],
            recv_sem=in_rsem.at[a, sem_at],
            device_id={"dev": d},
            device_id_type=MESH,
        )

    def keys_in(d, slot, sem_at):
        return pltpu.make_async_remote_copy(
            src_ref=send.at[pl.ds(1, 2), head_rows(d)],
            dst_ref=recv.at[pl.ds(1, 2), slot],
            send_sem=in_ssem.at[1, d],
            recv_sem=in_rsem.at[1, sem_at],
            device_id={"dev": d},
            device_id_type=MESH,
        )

    def nth_peer(i):
        return lax.rem(me + 5 * i, n_dev)

    def send_keys(i, carry):
        keys_in(nth_peer(i), me, me).start()
        return carry

    to_features(1)
    to_features(2)
    pl.semaphore_wait(barrier, n_dev + 1)
    lax.fori_loop(1, n_dev, send_keys, 0)
    to_features(0)

    def send_queries(i, carry):
        d = nth_peer(i)
        keys_in(d, me, me).wait_send()
        in_copy(0, d, me, me).start()
        return carry

    lax.fori_loop(1, n_dev, send_queries, 0)

    acc[...] = jnp.zeros_like(acc)

    def place(a, block, piece):
        feat[a - 1, :, frame_cols(block, frames)] = piece
        rows[a - 1, frame_cols(block, frames), :] = transposed(piece)

    def gather(i, carry):
        src = lax.rem(me - i + n_dev, n_dev)

        @pl.when(i > 0)
        def _():
            keys_in(src, src, src).wait_recv()

        for a in (1, 2):
            place(a, src + far_blocks, recv[a, src])
        return carry

    lax.fori_loop(0, n_dev, gather, 0)

    def halo_copy(a):
        return pltpu.make_async_remote_copy(
            src_ref=recv.at[a, pl.ds(n_dev - far_blocks, far_blocks)],
            dst_ref=halo.at[a - 1],
            send_sem=halo_ssem.at[a - 1],
            recv_sem=halo_rsem.at[a - 1],
            device_id={"seg": next_seg},
            device_id_type=MESH,
        )

    for a in (1, 2):
        halo_copy(a).start()

    def out_copy(a, d, sem_at, head):
        return pltpu.make_async_remote_copy(
            src_ref=out_send.at[a, d],
            dst_ref=out_recv.at[a, head_rows(head)],
            send_sem=out_ssem.at[a, d],
            recv_sem=out_rsem.at[a, sem_at],
            device_id={"dev": d},
            device_id_type=MESH,
        )

    def give(a, block, value):
        @pl.when(block == me)
        def _():
            out_recv[a, head_rows(me), :] = value

        @pl.when(block != me)
        def _():
            out_send[a, block] = value
            out_copy(a, block, me, me).start()

    def keys_out(d, sem_at, head):
        return pltpu.make_async_remote_copy(
            src_ref=out_send.at[pl.ds(1, 2), d],
            dst_ref=out_recv.at[pl.ds(1, 2), head_rows(head)],
            send_sem=out_ssem.at[1, d],
            recv_sem=out_rsem.at[1, sem_at],
            device_id={"dev": d},
            device_id_type=MESH,
        )

    def give_keys(block):
        @pl.when(block == me)
        def _():
            for a in (1, 2):
                out_recv[a, head_rows(me), :] = acc[a - 1, block + far_blocks].astype(BF16)

        @pl.when(block != me)
        def _():
            for a in (1, 2):
                out_send[a, block] = acc[a - 1, block + far_blocks].astype(BF16)
            keys_out(block, me, me).start()

    def far_copy():
        return pltpu.make_async_remote_copy(
            src_ref=far_out,
            dst_ref=far_in,
            send_sem=far_ssem,
            recv_sem=far_rsem,
            device_id={"seg": prev_seg},
            device_id_type=MESH,
        )

    key_at = lax.broadcasted_iota(jnp.int32, (ext, frames), 0)
    query_at = lax.broadcasted_iota(jnp.int32, (ext, frames), 1)
    in_window = (key_at >= query_at) & (key_at <= query_at + WINDOW)

    def one_block(s, carry):
        block = lax.rem(me - s + n_dev, n_dev)

        @pl.when(s > 0)
        def _():
            in_copy(0, block, block, block).wait_recv()

        @pl.when(s == jnp.maximum(me - far_blocks + 1, 0))
        def _():
            for a in (1, 2):
                halo_copy(a).wait_recv()
                for b in range(far_blocks):
                    place(a, b, halo[a - 1, b])

        q_feat = recv[0, block]
        scores = jnp.dot(
            rows[0, WINDOW : WINDOW + segment, :], q_feat, preferred_element_type=F32
        ) * (factor * LOG2E)
        numer = jnp.exp2(scores - scores.max(0, keepdims=True))
        total = numer.sum(0, keepdims=True)
        summed = jnp.dot(
            feat[1, :, WINDOW : WINDOW + segment], numer.astype(BF16), preferred_element_type=F32
        )
        target = (summed / total).astype(BF16).astype(F32)

        span = frame_cols(block, ext)
        first = (seg * n_dev + block) * frames - WINDOW
        allowed = in_window & (key_at + first >= 0)
        near = jnp.dot(rows[0, span, :], q_feat, preferred_element_type=F32) * (factor * LOG2E)
        near = jnp.where(allowed, near, -1e30)
        near_numer = jnp.exp2(near - near.max(0, keepdims=True))
        prob = near_numer / near_numer.sum(0, keepdims=True)
        weights = prob.astype(BF16)
        student = jnp.dot(feat[1, :, span], weights, preferred_element_type=F32)
        d_out = (128.0 * (student - target)).astype(BF16)
        d_prob = jnp.dot(rows[1, span, :], d_out, preferred_element_type=F32)
        inner = (prob * d_prob).sum(0, keepdims=True)
        d_scores = (prob * (d_prob - inner) * factor).astype(BF16)
        grad_q = jnp.dot(feat[0, :, span], d_scores, preferred_element_type=F32)
        grad_k = lax.dot_general(q_feat, d_scores, CONTRACT_LANES, preferred_element_type=F32)
        grad_v = lax.dot_general(d_out, weights, CONTRACT_LANES, preferred_element_type=F32)
        for b in range(far_blocks + 1):
            cols = slice(b * frames, (b + 1) * frames)
            acc[0, block + b] += grad_k[:, cols]
            acc[1, block + b] += grad_v[:, cols]
        give(0, block, grad_q.astype(BF16))

        last_first = jnp.where(me >= far_blocks - 1, 0, me + 1)

        @pl.when(block == last_first)
        def _():
            far_out[...] = acc[:, 0:far_blocks].astype(BF16)
            far_copy().start()

        @pl.when((s >= far_blocks) & (block < n_dev - far_blocks))
        def _():
            give_keys(block)

        return carry

    lax.fori_loop(0, n_dev, one_block, 0)

    for s in range(far_blocks):
        block = lax.rem(me - s + n_dev, n_dev)

        @pl.when(block < n_dev - far_blocks)
        def _():
            give_keys(block)

    far_copy().wait_recv()
    for b in range(far_blocks):
        for a in range(2):
            acc[a, n_dev + b] += far_in[a, b].astype(F32)
        give_keys(n_dev - far_blocks + b)

    group = 384 // dim
    for a, out in ((0, gq_ref), (1, gk_ref), (2, gv_ref)):
        for g in range(n_dev // group):
            for i in range(group):
                head = g * group + i

                @pl.when(head != me)
                def _():
                    if a == 0:
                        out_copy(a, head, head, head).wait_recv()
                    elif a == 1:
                        keys_out(head, head, head).wait_recv()

            for t in range(3 * g, 3 * g + 3):
                cols = slice(t * 128, (t + 1) * 128)
                out[:, cols] = transposed(out_recv[a, cols, :])

    def drain(i, carry):
        d = lax.rem(me + i, n_dev)
        in_copy(0, d, me, me).wait_send()
        out_copy(0, d, me, me).wait_send()
        keys_out(d, me, me).wait_send()
        return carry

    lax.fori_loop(1, n_dev, drain, 0)
    for a in (1, 2):
        halo_copy(a).wait_send()
    far_copy().wait_send()


def local(n_dev, n_seg, queries, keys, values):
    frames, width = queries.shape
    dim = width // n_dev
    far_blocks = WINDOW // frames
    held = n_dev + far_blocks
    vmem = pl.BlockSpec(memory_space=pltpu.VMEM)
    dma = pltpu.SemaphoreType.DMA
    return pl.pallas_call(
        functools.partial(kernel, n_dev, n_seg),
        out_shape=[jax.ShapeDtypeStruct((frames, width), BF16)] * 3,
        in_specs=[pl.BlockSpec(memory_space=pltpu.HBM)] * 3,
        out_specs=[vmem] * 3,
        scratch_shapes=[
            pltpu.VMEM((3, frames, width), BF16),
            pltpu.VMEM((3, width, frames), BF16),
            pltpu.VMEM((3, n_dev, dim, frames), BF16),
            pltpu.VMEM((2, far_blocks, dim, frames), BF16),
            pltpu.VMEM((2, dim, held * frames), BF16),
            pltpu.VMEM((2, held * frames, dim), BF16),
            pltpu.VMEM((2, held, dim, frames), F32),
            pltpu.VMEM((2, far_blocks, dim, frames), BF16),
            pltpu.VMEM((2, far_blocks, dim, frames), BF16),
            pltpu.VMEM((3, n_dev, dim, frames), BF16),
            pltpu.VMEM((3, width, frames), BF16),
            dma((3, n_dev)),
            dma((3, n_dev)),
            dma((2,)),
            dma((2,)),
            dma,
            dma,
            dma((3, n_dev)),
            dma((3, n_dev)),
            dma((3,)),
        ],
        compiler_params=pltpu.CompilerParams(
            collective_id=0, has_side_effects=True, vmem_limit_bytes=48 << 20
        ),
        name="heads_exchange",
    )(queries, keys, values)


def solution(mesh):
    n_dev, n_seg = mesh.shape["dev"], mesh.shape["seg"]
    rows = P(("seg", "dev"), None)
    return jax.shard_map(
        functools.partial(local, n_dev, n_seg),
        mesh=mesh,
        in_specs=(rows, rows, rows),
        out_specs=(rows, rows, rows),
        check_vma=False,
    )
```

```python
import functools

import jax
import jax.numpy as jnp
from jax import lax
from jax.experimental import pallas as pl
from jax.experimental.pallas import tpu as pltpu
from jax.sharding import PartitionSpec as P

HEADS = 16
WINDOW = 256
MESH = pl.DeviceIdType.MESH
F32 = jnp.float32
BF16 = jnp.bfloat16
LOG2E = 1.4426950408889634
CONTRACT_LANES = (((1,), (1,)), ((), ()))


def transposed(tile):
    return tile.T


def kernel(
    n_dev,
    n_seg,
    q_ref,
    k_ref,
    v_ref,
    out_recv,
    held_in,
    send,
    recv,
    halo,
    feat,
    rows,
    acc,
    far_out,
    far_in,
    out_send,
    in_ssem,
    in_rsem,
    halo_ssem,
    halo_rsem,
    far_ssem,
    far_rsem,
    out_ssem,
    out_rsem,
    load_sem,
    own_sem,
):
    me = lax.axis_index("dev")
    seg = lax.axis_index("seg")
    frames, width = q_ref.shape
    loads = [
        pltpu.make_async_copy(ref, held_in.at[a], load_sem.at[a])
        for a, ref in ((0, q_ref), (1, k_ref), (2, v_ref))
    ]
    for a in (1, 2, 0):
        loads[a].start()
    dim = width // n_dev
    far_blocks = WINDOW // frames
    segment = n_dev * frames
    ext = WINDOW + frames
    factor = dim ** (-0.5)
    next_seg = lax.rem(seg + 1, n_seg)
    prev_seg = lax.rem(seg + n_seg - 1, n_seg)
    tiles = width // 128

    def head_rows(d):
        return pl.ds(pl.multiple_of(d * dim, 32), dim)

    def frame_cols(block, count):
        return pl.ds(pl.multiple_of(block * frames, 128), count)

    barrier = pltpu.get_barrier_semaphore()
    for i in range(1, n_dev):
        pl.semaphore_signal(
            barrier, inc=1, device_id={"dev": lax.rem(me + i, n_dev)}, device_id_type=MESH
        )
    pl.semaphore_signal(barrier, inc=1, device_id={"seg": next_seg}, device_id_type=MESH)
    pl.semaphore_signal(barrier, inc=1, device_id={"seg": prev_seg}, device_id_type=MESH)

    def to_features(a):
        loads[a].wait()
        for t in range(tiles):
            cols = slice(t * 128, (t + 1) * 128)
            send[a, cols, :] = transposed(held_in[a, :, cols])
        recv[a, me] = send[a, head_rows(me), :]

    def in_copy(a, d, slot, sem_at):
        return pltpu.make_async_remote_copy(
            src_ref=send.at[a, head_rows(d)],
            dst_ref=recv.at[a, slot],
            send_sem=in_ssem.at[a, d],
            recv_sem=in_rsem.at[a, sem_at],
            device_id={"dev": d},
            device_id_type=MESH,
        )

    def keys_in(d, slot, sem_at):
        return pltpu.make_async_remote_copy(
            src_ref=send.at[pl.ds(1, 2), head_rows(d)],
            dst_ref=recv.at[pl.ds(1, 2), slot],
            send_sem=in_ssem.at[1, d],
            recv_sem=in_rsem.at[1, sem_at],
            device_id={"dev": d},
            device_id_type=MESH,
        )

    def nth_peer(i):
        return lax.rem(me + 5 * i, n_dev)

    def send_keys(i, carry):
        keys_in(nth_peer(i), me, me).start()
        return carry

    to_features(1)
    to_features(2)
    pl.semaphore_wait(barrier, n_dev + 1)
    lax.fori_loop(1, n_dev, send_keys, 0)
    to_features(0)

    def send_queries(i, carry):
        d = nth_peer(i)
        keys_in(d, me, me).wait_send()
        in_copy(0, d, me, me).start()
        return carry

    lax.fori_loop(1, n_dev, send_queries, 0)

    acc[...] = jnp.zeros_like(acc)

    def place(a, block, piece):
        feat[a - 1, :, frame_cols(block, frames)] = piece
        rows[a - 1, frame_cols(block, frames), :] = transposed(piece)

    def gather(i, carry):
        src = lax.rem(me - i + n_dev, n_dev)

        @pl.when(i > 0)
        def _():
            keys_in(src, src, src).wait_recv()

        for a in (1, 2):
            place(a, src + far_blocks, recv[a, src])
        return carry

    lax.fori_loop(0, n_dev, gather, 0)

    def halo_copy(a):
        return pltpu.make_async_remote_copy(
            src_ref=recv.at[a, pl.ds(n_dev - far_blocks, far_blocks)],
            dst_ref=halo.at[a - 1],
            send_sem=halo_ssem.at[a - 1],
            recv_sem=halo_rsem.at[a - 1],
            device_id={"seg": next_seg},
            device_id_type=MESH,
        )

    for a in (1, 2):
        halo_copy(a).start()

    def out_copy(a, d, sem_at, head):
        return pltpu.make_async_remote_copy(
            src_ref=out_send.at[a, d],
            dst_ref=out_recv.at[a, head_rows(head)],
            send_sem=out_ssem.at[a, d],
            recv_sem=out_rsem.at[a, sem_at],
            device_id={"dev": d},
            device_id_type=MESH,
        )

    def own_copy(a):
        return pltpu.make_async_copy(
            out_send.at[a, me], out_recv.at[a, head_rows(me)], own_sem.at[a]
        )

    def give(a, block, value):
        out_send[a, block] = value

        @pl.when(block == me)
        def _():
            own_copy(a).start()

        @pl.when(block != me)
        def _():
            out_copy(a, block, me, me).start()

    def keys_out(d, sem_at, head):
        return pltpu.make_async_remote_copy(
            src_ref=out_send.at[pl.ds(1, 2), d],
            dst_ref=out_recv.at[pl.ds(1, 2), head_rows(head)],
            send_sem=out_ssem.at[1, d],
            recv_sem=out_rsem.at[1, sem_at],
            device_id={"dev": d},
            device_id_type=MESH,
        )

    def give_keys(block):
        for a in (1, 2):
            out_send[a, block] = acc[a - 1, block + far_blocks].astype(BF16)

        @pl.when(block == me)
        def _():
            for a in (1, 2):
                own_copy(a).start()

        @pl.when(block != me)
        def _():
            keys_out(block, me, me).start()

    def far_copy():
        return pltpu.make_async_remote_copy(
            src_ref=far_out,
            dst_ref=far_in,
            send_sem=far_ssem,
            recv_sem=far_rsem,
            device_id={"seg": prev_seg},
            device_id_type=MESH,
        )

    key_at = lax.broadcasted_iota(jnp.int32, (ext, frames), 0)
    query_at = lax.broadcasted_iota(jnp.int32, (ext, frames), 1)
    in_window = (key_at >= query_at) & (key_at <= query_at + WINDOW)

    def one_block(s, carry):
        block = lax.rem(me - s + n_dev, n_dev)

        @pl.when(s > 0)
        def _():
            in_copy(0, block, block, block).wait_recv()

        @pl.when(s == jnp.maximum(me - far_blocks + 1, 0))
        def _():
            for a in (1, 2):
                halo_copy(a).wait_recv()
                for b in range(far_blocks):
                    place(a, b, halo[a - 1, b])

        q_feat = recv[0, block]
        scores = jnp.dot(
            rows[0, WINDOW : WINDOW + segment, :], q_feat, preferred_element_type=F32
        ) * (factor * LOG2E)
        numer = jnp.exp2(scores - scores.max(0, keepdims=True))
        total = numer.sum(0, keepdims=True)
        summed = jnp.dot(
            feat[1, :, WINDOW : WINDOW + segment], numer.astype(BF16), preferred_element_type=F32
        )
        target = (summed / total).astype(BF16).astype(F32)

        span = frame_cols(block, ext)
        first = (seg * n_dev + block) * frames - WINDOW
        allowed = in_window & (key_at + first >= 0)
        near = jnp.dot(rows[0, span, :], q_feat, preferred_element_type=F32) * (factor * LOG2E)
        near = jnp.where(allowed, near, -1e30)
        near_numer = jnp.exp2(near - near.max(0, keepdims=True))
        prob = near_numer / near_numer.sum(0, keepdims=True)
        weights = prob.astype(BF16)
        student = jnp.dot(feat[1, :, span], weights, preferred_element_type=F32)
        d_out = (128.0 * (student - target)).astype(BF16)
        d_prob = jnp.dot(rows[1, span, :], d_out, preferred_element_type=F32)
        inner = (prob * d_prob).sum(0, keepdims=True)
        d_scores = (prob * (d_prob - inner) * factor).astype(BF16)
        grad_q = jnp.dot(feat[0, :, span], d_scores, preferred_element_type=F32)
        grad_k = lax.dot_general(q_feat, d_scores, CONTRACT_LANES, preferred_element_type=F32)
        grad_v = lax.dot_general(d_out, weights, CONTRACT_LANES, preferred_element_type=F32)
        for b in range(far_blocks + 1):
            cols = slice(b * frames, (b + 1) * frames)
            acc[0, block + b] += grad_k[:, cols]
            acc[1, block + b] += grad_v[:, cols]
        give(0, block, grad_q.astype(BF16))

        last_first = jnp.where(me >= far_blocks - 1, 0, me + 1)

        @pl.when(block == last_first)
        def _():
            far_out[...] = acc[:, 0:far_blocks].astype(BF16)
            far_copy().start()

        @pl.when((s >= far_blocks) & (block < n_dev - far_blocks))
        def _():
            give_keys(block)

        return carry

    lax.fori_loop(0, n_dev, one_block, 0)

    for s in range(far_blocks):
        block = lax.rem(me - s + n_dev, n_dev)

        @pl.when(block < n_dev - far_blocks)
        def _():
            give_keys(block)

    far_copy().wait_recv()
    for b in range(far_blocks):
        for a in range(2):
            acc[a, n_dev + b] += far_in[a, b].astype(F32)
        give_keys(n_dev - far_blocks + b)

    def drain(i, carry):
        d = lax.rem(me + i, n_dev)
        in_copy(0, d, me, me).wait_send()
        out_copy(0, d, me, me).wait_send()
        keys_out(d, me, me).wait_send()
        out_copy(0, d, d, d).wait_recv()
        keys_out(d, d, d).wait_recv()
        return carry

    lax.fori_loop(1, n_dev, drain, 0)
    for a in (1, 2):
        halo_copy(a).wait_send()
    far_copy().wait_send()
    for a in range(3):
        own_copy(a).wait()


def to_frames(feat_ref, gq_ref, gk_ref, gv_ref, feat, held, load_sem, store_sem):
    outs = (gq_ref, gk_ref, gv_ref)
    loads = [
        pltpu.make_async_copy(feat_ref.at[a], feat.at[a], load_sem.at[a]) for a in range(3)
    ]
    stores = [pltpu.make_async_copy(held.at[a], outs[a], store_sem.at[a]) for a in range(3)]
    for load in loads:
        load.start()
    for a in range(3):
        loads[a].wait()
        for t in range(feat.shape[1] // 128):
            cols = slice(t * 128, (t + 1) * 128)
            held[a, :, cols] = transposed(feat[a, cols, :])
        stores[a].start()
    for store in stores:
        store.wait()


def local(n_dev, n_seg, queries, keys, values):
    frames, width = queries.shape
    dim = width // n_dev
    far_blocks = WINDOW // frames
    held = n_dev + far_blocks
    dma = pltpu.SemaphoreType.DMA
    hbm = pl.BlockSpec(memory_space=pltpu.HBM)
    grads = pl.pallas_call(
        functools.partial(kernel, n_dev, n_seg),
        out_shape=jax.ShapeDtypeStruct((3, width, frames), BF16),
        in_specs=[hbm] * 3,
        out_specs=hbm,
        scratch_shapes=[
            pltpu.VMEM((3, frames, width), BF16),
            pltpu.VMEM((3, width, frames), BF16),
            pltpu.VMEM((3, n_dev, dim, frames), BF16),
            pltpu.VMEM((2, far_blocks, dim, frames), BF16),
            pltpu.VMEM((2, dim, held * frames), BF16),
            pltpu.VMEM((2, held * frames, dim), BF16),
            pltpu.VMEM((2, held, dim, frames), F32),
            pltpu.VMEM((2, far_blocks, dim, frames), BF16),
            pltpu.VMEM((2, far_blocks, dim, frames), BF16),
            pltpu.VMEM((3, n_dev, dim, frames), BF16),
            dma((3, n_dev)),
            dma((3, n_dev)),
            dma((2,)),
            dma((2,)),
            dma,
            dma,
            dma((3, n_dev)),
            dma((3, n_dev)),
            dma((3,)),
            dma((3,)),
        ],
        compiler_params=pltpu.CompilerParams(
            collective_id=0, has_side_effects=True, vmem_limit_bytes=60 << 20
        ),
        name="heads_exchange",
    )(queries, keys, values)
    return pl.pallas_call(
        to_frames,
        out_shape=[jax.ShapeDtypeStruct((frames, width), BF16)] * 3,
        in_specs=[hbm],
        out_specs=[hbm] * 3,
        scratch_shapes=[
            pltpu.VMEM((3, width, frames), BF16),
            pltpu.VMEM((3, frames, width), BF16),
            dma((3,)),
            dma((3,)),
        ],
        compiler_params=pltpu.CompilerParams(vmem_limit_bytes=60 << 20),
        name="to_frames",
    )(grads)


def solution(mesh):
    n_dev, n_seg = mesh.shape["dev"], mesh.shape["seg"]
    rows = P(("seg", "dev"), None)
    return jax.shard_map(
        functools.partial(local, n_dev, n_seg),
        mesh=mesh,
        in_specs=(rows, rows, rows),
        out_specs=(rows, rows, rows),
        check_vma=False,
    )
```

```python
import functools

import jax
import jax.numpy as jnp
from jax import lax
from jax.experimental import pallas as pl
from jax.experimental.pallas import tpu as pltpu
from jax.sharding import PartitionSpec as P

HEADS = 16
WINDOW = 256
MESH = pl.DeviceIdType.MESH
F32 = jnp.float32
BF16 = jnp.bfloat16
LOG2E = 1.4426950408889634
CONTRACT_LANES = (((1,), (1,)), ((), ()))


def transposed(tile):
    return tile.T


def kernel(
    n_dev,
    n_seg,
    q_ref,
    k_ref,
    v_ref,
    out_recv,
    held_in,
    send,
    recv,
    halo,
    feat,
    rows,
    acc,
    far_out,
    far_in,
    out_send,
    in_ssem,
    in_rsem,
    halo_ssem,
    halo_rsem,
    far_ssem,
    far_rsem,
    out_ssem,
    out_rsem,
    load_sem,
    own_sem,
):
    me = lax.axis_index("dev")
    seg = lax.axis_index("seg")
    frames, width = q_ref.shape
    loads = [
        pltpu.make_async_copy(ref, held_in.at[a], load_sem.at[a])
        for a, ref in ((0, q_ref), (1, k_ref), (2, v_ref))
    ]
    for a in (1, 2, 0):
        loads[a].start()
    dim = width // n_dev
    far_blocks = WINDOW // frames
    segment = n_dev * frames
    ext = WINDOW + frames
    factor = dim ** (-0.5)
    next_seg = lax.rem(seg + 1, n_seg)
    prev_seg = lax.rem(seg + n_seg - 1, n_seg)
    tiles = width // 128

    def head_rows(d):
        return pl.ds(pl.multiple_of(d * dim, 32), dim)

    def frame_cols(block, count):
        return pl.ds(pl.multiple_of(block * frames, 128), count)

    barrier = pltpu.get_barrier_semaphore()
    for i in range(1, n_dev):
        pl.semaphore_signal(
            barrier, inc=1, device_id={"dev": lax.rem(me + i, n_dev)}, device_id_type=MESH
        )
    pl.semaphore_signal(barrier, inc=1, device_id={"seg": next_seg}, device_id_type=MESH)
    pl.semaphore_signal(barrier, inc=1, device_id={"seg": prev_seg}, device_id_type=MESH)

    def to_features(a):
        loads[a].wait()
        for t in range(tiles):
            cols = slice(t * 128, (t + 1) * 128)
            send[a, cols, :] = transposed(held_in[a, :, cols])
        recv[a, me] = send[a, head_rows(me), :]

    def in_copy(a, d, slot, sem_at):
        return pltpu.make_async_remote_copy(
            src_ref=send.at[a, head_rows(d)],
            dst_ref=recv.at[a, slot],
            send_sem=in_ssem.at[a, d],
            recv_sem=in_rsem.at[a, sem_at],
            device_id={"dev": d},
            device_id_type=MESH,
        )

    def nth_peer(i):
        return lax.rem(me + 5 * i, n_dev)

    def send_in(a):
        def body(i, carry):
            in_copy(a, nth_peer(i), me, me).start()
            return carry

        lax.fori_loop(1, n_dev, body, 0)

    to_features(1)
    pl.semaphore_wait(barrier, n_dev + 1)
    send_in(1)
    to_features(2)
    send_in(2)
    to_features(0)

    def send_queries(i, carry):
        d = nth_peer(i)
        for a in (1, 2):
            in_copy(a, d, me, me).wait_send()
        in_copy(0, d, me, me).start()
        return carry

    lax.fori_loop(1, n_dev, send_queries, 0)

    acc[...] = jnp.zeros_like(acc)

    def place(a, block, piece):
        feat[a - 1, :, frame_cols(block, frames)] = piece
        rows[a - 1, frame_cols(block, frames), :] = transposed(piece)

    def gather(i, carry):
        src = lax.rem(me - i + n_dev, n_dev)

        @pl.when(i > 0)
        def _():
            for a in (1, 2):
                in_copy(a, src, src, src).wait_recv()

        for a in (1, 2):
            place(a, src + far_blocks, recv[a, src])
        return carry

    lax.fori_loop(0, n_dev, gather, 0)

    def halo_copy(a):
        return pltpu.make_async_remote_copy(
            src_ref=recv.at[a, pl.ds(n_dev - far_blocks, far_blocks)],
            dst_ref=halo.at[a - 1],
            send_sem=halo_ssem.at[a - 1],
            recv_sem=halo_rsem.at[a - 1],
            device_id={"seg": next_seg},
            device_id_type=MESH,
        )

    for a in (1, 2):
        halo_copy(a).start()

    def out_copy(a, d, sem_at, head):
        return pltpu.make_async_remote_copy(
            src_ref=out_send.at[a, d],
            dst_ref=out_recv.at[a, head_rows(head)],
            send_sem=out_ssem.at[a, d],
            recv_sem=out_rsem.at[a, sem_at],
            device_id={"dev": d},
            device_id_type=MESH,
        )

    def own_copy(a):
        return pltpu.make_async_copy(
            out_send.at[a, me], out_recv.at[a, head_rows(me)], own_sem.at[a]
        )

    def give(a, block, value):
        out_send[a, block] = value

        @pl.when(block == me)
        def _():
            own_copy(a).start()

        @pl.when(block != me)
        def _():
            out_copy(a, block, me, me).start()

    def keys_out(d, sem_at, head):
        return pltpu.make_async_remote_copy(
            src_ref=out_send.at[pl.ds(1, 2), d],
            dst_ref=out_recv.at[pl.ds(1, 2), head_rows(head)],
            send_sem=out_ssem.at[1, d],
            recv_sem=out_rsem.at[1, sem_at],
            device_id={"dev": d},
            device_id_type=MESH,
        )

    def give_keys(block):
        for a in (1, 2):
            out_send[a, block] = acc[a - 1, block + far_blocks].astype(BF16)

        @pl.when(block == me)
        def _():
            for a in (1, 2):
                own_copy(a).start()

        @pl.when(block != me)
        def _():
            keys_out(block, me, me).start()

    def far_copy():
        return pltpu.make_async_remote_copy(
            src_ref=far_out,
            dst_ref=far_in,
            send_sem=far_ssem,
            recv_sem=far_rsem,
            device_id={"seg": prev_seg},
            device_id_type=MESH,
        )

    key_at = lax.broadcasted_iota(jnp.int32, (ext, frames), 0)
    query_at = lax.broadcasted_iota(jnp.int32, (ext, frames), 1)
    in_window = (key_at >= query_at) & (key_at <= query_at + WINDOW)

    def one_block(s, carry):
        block = lax.rem(me - s + n_dev, n_dev)

        @pl.when(s > 0)
        def _():
            in_copy(0, block, block, block).wait_recv()

        @pl.when(s == jnp.maximum(me - far_blocks + 1, 0))
        def _():
            for a in (1, 2):
                halo_copy(a).wait_recv()
                for b in range(far_blocks):
                    place(a, b, halo[a - 1, b])

        q_feat = recv[0, block]
        scores = jnp.dot(
            rows[0, WINDOW : WINDOW + segment, :], q_feat, preferred_element_type=F32
        ) * (factor * LOG2E)
        numer = jnp.exp2(scores - scores.max(0, keepdims=True))
        total = numer.sum(0, keepdims=True)
        summed = jnp.dot(
            feat[1, :, WINDOW : WINDOW + segment], numer.astype(BF16), preferred_element_type=F32
        )
        target = (summed / total).astype(BF16).astype(F32)

        span = frame_cols(block, ext)
        first = (seg * n_dev + block) * frames - WINDOW
        allowed = in_window & (key_at + first >= 0)
        near = jnp.dot(rows[0, span, :], q_feat, preferred_element_type=F32) * (factor * LOG2E)
        near = jnp.where(allowed, near, -1e30)
        near_numer = jnp.exp2(near - near.max(0, keepdims=True))
        prob = near_numer / near_numer.sum(0, keepdims=True)
        weights = prob.astype(BF16)
        student = jnp.dot(feat[1, :, span], weights, preferred_element_type=F32)
        d_out = (128.0 * (student - target)).astype(BF16)
        d_prob = jnp.dot(rows[1, span, :], d_out, preferred_element_type=F32)
        inner = (prob * d_prob).sum(0, keepdims=True)
        d_scores = (prob * (d_prob - inner) * factor).astype(BF16)
        grad_q = jnp.dot(feat[0, :, span], d_scores, preferred_element_type=F32)
        grad_k = lax.dot_general(q_feat, d_scores, CONTRACT_LANES, preferred_element_type=F32)
        grad_v = lax.dot_general(d_out, weights, CONTRACT_LANES, preferred_element_type=F32)
        for b in range(far_blocks + 1):
            cols = slice(b * frames, (b + 1) * frames)
            acc[0, block + b] += grad_k[:, cols]
            acc[1, block + b] += grad_v[:, cols]
        give(0, block, grad_q.astype(BF16))

        last_first = jnp.where(me >= far_blocks - 1, 0, me + 1)

        @pl.when(block == last_first)
        def _():
            far_out[...] = acc[:, 0:far_blocks].astype(BF16)
            far_copy().start()

        @pl.when((s >= far_blocks) & (block < n_dev - far_blocks))
        def _():
            give_keys(block)

        return carry

    lax.fori_loop(0, n_dev, one_block, 0)

    for s in range(far_blocks):
        block = lax.rem(me - s + n_dev, n_dev)

        @pl.when(block < n_dev - far_blocks)
        def _():
            give_keys(block)

    far_copy().wait_recv()
    for b in range(far_blocks):
        for a in range(2):
            acc[a, n_dev + b] += far_in[a, b].astype(F32)
        give_keys(n_dev - far_blocks + b)

    def drain(i, carry):
        d = lax.rem(me + i, n_dev)
        in_copy(0, d, me, me).wait_send()
        out_copy(0, d, me, me).wait_send()
        keys_out(d, me, me).wait_send()
        out_copy(0, d, d, d).wait_recv()
        keys_out(d, d, d).wait_recv()
        return carry

    lax.fori_loop(1, n_dev, drain, 0)
    for a in (1, 2):
        halo_copy(a).wait_send()
    far_copy().wait_send()
    for a in range(3):
        own_copy(a).wait()


def to_frames(feat_ref, gq_ref, gk_ref, gv_ref, feat, held, load_sem, store_sem):
    outs = (gq_ref, gk_ref, gv_ref)
    loads = [
        pltpu.make_async_copy(feat_ref.at[a], feat.at[a], load_sem.at[a]) for a in range(3)
    ]
    stores = [pltpu.make_async_copy(held.at[a], outs[a], store_sem.at[a]) for a in range(3)]
    for load in loads:
        load.start()
    for a in range(3):
        loads[a].wait()
        for t in range(feat.shape[1] // 128):
            cols = slice(t * 128, (t + 1) * 128)
            held[a, :, cols] = transposed(feat[a, cols, :])
        stores[a].start()
    for store in stores:
        store.wait()


def local(n_dev, n_seg, queries, keys, values):
    frames, width = queries.shape
    dim = width // n_dev
    far_blocks = WINDOW // frames
    held = n_dev + far_blocks
    dma = pltpu.SemaphoreType.DMA
    hbm = pl.BlockSpec(memory_space=pltpu.HBM)
    grads = pl.pallas_call(
        functools.partial(kernel, n_dev, n_seg),
        out_shape=jax.ShapeDtypeStruct((3, width, frames), BF16),
        in_specs=[hbm] * 3,
        out_specs=hbm,
        scratch_shapes=[
            pltpu.VMEM((3, frames, width), BF16),
            pltpu.VMEM((3, width, frames), BF16),
            pltpu.VMEM((3, n_dev, dim, frames), BF16),
            pltpu.VMEM((2, far_blocks, dim, frames), BF16),
            pltpu.VMEM((2, dim, held * frames), BF16),
            pltpu.VMEM((2, held * frames, dim), BF16),
            pltpu.VMEM((2, held, dim, frames), F32),
            pltpu.VMEM((2, far_blocks, dim, frames), BF16),
            pltpu.VMEM((2, far_blocks, dim, frames), BF16),
            pltpu.VMEM((3, n_dev, dim, frames), BF16),
            dma((3, n_dev)),
            dma((3, n_dev)),
            dma((2,)),
            dma((2,)),
            dma,
            dma,
            dma((3, n_dev)),
            dma((3, n_dev)),
            dma((3,)),
            dma((3,)),
        ],
        compiler_params=pltpu.CompilerParams(
            collective_id=0, has_side_effects=True, vmem_limit_bytes=60 << 20
        ),
        name="heads_exchange",
    )(queries, keys, values)
    return pl.pallas_call(
        to_frames,
        out_shape=[jax.ShapeDtypeStruct((frames, width), BF16)] * 3,
        in_specs=[hbm],
        out_specs=[hbm] * 3,
        scratch_shapes=[
            pltpu.VMEM((3, width, frames), BF16),
            pltpu.VMEM((3, frames, width), BF16),
            dma((3,)),
            dma((3,)),
        ],
        compiler_params=pltpu.CompilerParams(vmem_limit_bytes=60 << 20),
        name="to_frames",
    )(grads)


def solution(mesh):
    n_dev, n_seg = mesh.shape["dev"], mesh.shape["seg"]
    rows = P(("seg", "dev"), None)
    return jax.shard_map(
        functools.partial(local, n_dev, n_seg),
        mesh=mesh,
        in_specs=(rows, rows, rows),
        out_specs=(rows, rows, rows),
        check_vma=False,
    )
```
